128 devices in a mesh: tp: 8 (over z_hi, x), grp: 16 (over z_lo, y, core).
Axes of the slice: x: 4, y: 4, z: 4 (z_hi: 2, z_lo: 2; z = z_hi * 2 + z_lo), core: 2. Of those that a mesh axis runs over, the one named last changes fastest.
Arguments:
- queries: bfloat16 [16, 16, 16, 9216], P('grp', None, None, 'tp'), may hold values from -8 to 8
- responses: bfloat16 [16, 16, 16, 3072], P('grp', None, None, 'tp'), may hold values from -8 to 8
- cache_pool: bfloat16 [2048, 64, 3072], P('grp', None, 'tp'), may hold values from -8 to 8
- page_table: int32 [16, 64], P('grp'), may hold values from 0 to 127, as said below
- lengths: int32 [16, 16], replicated, may hold values from 8 to 16
- routes: int32 [16, 16, 1], P('grp'), may hold values from 0 to 15; in each aligned block of 16 rows (0 to 15, 16 to 31, ..., all dimensions but the last counted through in order) at most 2 rows name the same one
- student_rows: bfloat16 [16, 32, 16, 6144], P('grp'), may hold values from -6 to 6
- projection: bfloat16 [6144, 9216], P(None, 'tp'), may hold values from -0.078125 to 0.078125
Outputs:
- grad_proj: bfloat16 [6144, 9216], P('grp', 'tp')
The draws below stay inside these ranges and needn't reach their ends.
Inputs may be any that keep to these rules, and one draw needn't show every extreme that they name: `page_table`: each row names 64 different pages of its prompt's pool. `routes`: of the 16 responses of one prompt at most 2 go to one student group; every student group receives at least one response.
All inputs are finite; a program needn't handle non-finite values.
Results may differ from the reference program's by a relative error of at most 0.02.
Values may be sent and summed in bfloat16 or wider, within the bound.
No kernel may reach another device: no remote copies, remote signals or barrier semaphores. Data moves between devices by JAX's collectives and lax.ppermute only.
A program may use at most 128 MiB of HBM per device.

```python
import math
import jax
import jax.numpy as jnp
import numpy as np
from jax import lax

HQ = 48
KVH = 8
HD = 192
DS = 6144
PAGE = 64
R = 16
LMAX = 16
MOST = 2
GQA = 6
PRE_PAGES = 64
POOL_PAGES = 128
PROMPTS = 16
N_GRP = 16


def drawn_rows(key, shape, scale):
    return jax.random.truncated_normal(key, -3.0, 3.0, shape, jnp.float32) * scale


def draw_queries(key, part):
    key = jax.random.fold_in(key, 3)
    shape = (PROMPTS, R, LMAX, HQ * HD)
    values = drawn_rows(key, shape, 1.6)
    return values.astype(jnp.bfloat16)


def draw_responses(key, part):
    key = jax.random.fold_in(key, 5)
    shape = (PROMPTS, R, LMAX, KVH, HD)
    keys_part = drawn_rows(jax.random.fold_in(key, 10), shape, 2.5)
    values_part = drawn_rows(jax.random.fold_in(key, 20), shape, 1.0)
    stacked = jnp.stack([keys_part, values_part], axis=-2)
    return stacked.reshape(PROMPTS, R, LMAX, 2 * KVH * HD).astype(jnp.bfloat16)


def draw_cache_pool(key, part):
    key = jax.random.fold_in(key, 7)
    shape = (PROMPTS * POOL_PAGES, PAGE, KVH, HD)
    keys_part = drawn_rows(jax.random.fold_in(key, 10), shape, 1.6)
    values_part = drawn_rows(jax.random.fold_in(key, 20), shape, 1.0)
    stacked = jnp.stack([keys_part, values_part], axis=-2)
    return stacked.reshape(PROMPTS * POOL_PAGES, PAGE, 2 * KVH * HD).astype(jnp.bfloat16)


def draw_page_table(key, part):
    key = jax.random.fold_in(key, 11)
    prompt_keys = jax.random.split(key, PROMPTS)

    def one_row(row_key):
        return jax.random.permutation(row_key, POOL_PAGES)[:PRE_PAGES].astype(jnp.int32)
    return jax.vmap(one_row)(prompt_keys)


def draw_lengths(key, part):
    key = jax.random.fold_in(key, 13)
    first_key, second_key = jax.random.split(key)
    base = jax.random.randint(first_key, (PROMPTS, R), LMAX // 2, LMAX + 1).astype(jnp.int32)
    longest = jax.random.randint(second_key, (PROMPTS, 1), 0, R).astype(jnp.int32)
    return jnp.where(jnp.arange(R)[None, :] == longest, LMAX, base).astype(jnp.int32)


def block_levels(stream_key, shape, cuts, smallest, high):
    loudness, own = 1.0, jax.random.fold_in(stream_key, 6)
    for axis_at, parts in cuts:
        steps = jnp.exp(jax.random.uniform(jax.random.fold_in(own, axis_at), (parts,), jnp.float32, smallest / len(cuts), high / len(cuts)))
        loudness = loudness * jnp.repeat(steps, shape[axis_at] // parts).reshape([-1 if axis == axis_at else 1 for axis in range(len(shape))])
    return loudness


def assign_block(stream_key, own, number, rows, count, top, most, lean):
    ranking = jax.random.permutation(stream_key, count)
    packed, ordinary = load_shares(count, rows * top, most, lean, True), load_shares(count, rows * top, most, lean, False)
    places = jnp.arange(count)

    def named(sizes, turn):
        used = int((sizes > 0).sum())
        fixed = max(1, used // 4)
        passed = fixed + (places - fixed + turn * (used - fixed)) % max(1, count - fixed)
        return jnp.zeros((count,), jnp.int32).at[ranking[jnp.where(places < fixed, places, passed)]].set(jnp.asarray(sizes, jnp.int32))

    sizes = jnp.where(number % 4 == 0, named(packed, number // 4), named(ordinary, number - number // 4 - 1))
    mixed = jax.random.permutation(jax.random.fold_in(own, 3), count)
    source_of, sink = mixed[0:count // 2 * 2:2], mixed[1:count // 2 * 2:2]
    margin = jnp.minimum(sizes[source_of] - 1, most - sizes[sink]) // 2
    margin = jnp.where((source_of == ranking[0]) | (sink == ranking[0]) | (sizes[sink] == 0), 0, jnp.maximum(margin, 0))
    passed = jax.random.randint(jax.random.fold_in(own, 4), (count // 2,), 0, 1 << 20) % (margin + 1)
    sizes = sizes.at[source_of].add(-passed).at[sink].add(passed)
    members = jnp.searchsorted(jnp.cumsum(sizes), jnp.arange(rows * top), side="right").astype(jnp.int32)
    table = members.reshape(top, rows).T
    table = table[jax.random.permutation(jax.random.fold_in(own, 1), rows)]
    turn = jax.random.randint(jax.random.fold_in(own, 2), (rows, 1), 0, top)
    return jnp.take_along_axis(table, (jnp.arange(top)[None, :] + turn) % top, axis=1)


def load_shares(count, total, most, skew, full):
    loads = [(1 << 20) // math.isqrt(standing ** skew) + 1 for standing in range(1, count + 1)]
    largest = most if full else min(most, max(-(-total // count), total * loads[0] // sum(loads)))
    least = 1 if total - largest >= count - 1 else 0
    given, rest = [largest] + [least] * (count - 1), total - largest - least * (count - 1)
    while rest > 0:
        movable = [i for i in range(1, count) if given[i] < largest] or [i for i in range(1, count) if given[i] < most]
        whole, left = sum([loads[i] for i in movable]), rest
        for i in movable:
            addition = min(most - given[i], max(1, left * loads[i] // whole), rest)
            given[i] = given[i] + addition
            rest = rest - addition
    return np.array(given)


def bell_draw(key, extent, scale, reach, pieces=(), held_as=jnp.bfloat16):
    array = jax.random.normal(key, extent, jnp.float32) * scale
    if len(pieces) > 0:
        array = block_levels(key, extent, pieces, -0.22, 0.18) * array
    return jnp.clip(array, min=-reach, max=reach).astype(held_as)


def setup_inputs(seed: int = 0) -> dict:
    keys = jax.random.split(jax.random.key(seed), 9)
    queries = draw_queries(jax.random.fold_in(keys[8], 71), 0)
    responses = draw_responses(jax.random.fold_in(keys[8], 71), 0)
    cache_pool = draw_cache_pool(jax.random.fold_in(keys[8], 71), 0)
    page_table = draw_page_table(jax.random.fold_in(keys[8], 71), 0)
    lengths = draw_lengths(jax.random.fold_in(keys[8], 71), 0)
    routes_keys = jax.random.split(jax.random.fold_in(keys[5], 1), PROMPTS * R // R)
    routes_turns = jax.random.permutation(jax.random.fold_in(keys[5], 3), PROMPTS * R // R)
    routes = jax.vmap(lambda own, number: assign_block(jax.random.fold_in(keys[5], 2), own, number, R, N_GRP, 1, MOST, 2))(routes_keys, routes_turns).reshape((PROMPTS, R, 1))
    student_rows = bell_draw(keys[6], (PROMPTS, PROMPTS * MOST, LMAX, DS), 1.0, 6.0, ((0, 16),))
    projection = bell_draw(keys[7], (DS, HQ * HD), DS ** -0.5, 0.078125, ((1, 8),))
    return {"queries": queries, "responses": responses, "cache_pool": cache_pool, "page_table": page_table, "lengths": lengths, "routes": routes, "student_rows": student_rows, "projection": projection}


NEG_FILL = -1e30


def rounded(values):
    return lax.optimization_barrier(values.astype(jnp.bfloat16)).astype(jnp.float32)


def attention(query_rows, cache_resp, prefix):
    kv_heads = prefix.shape[-1] // (2 * HD)
    resp_count = query_rows.shape[0]
    resp_len = query_rows.shape[1]
    total_rows = resp_count * resp_len
    scaling = float(HD) ** -0.5
    grouped = query_rows.reshape(total_rows, kv_heads, GQA, HD).astype(jnp.float32)
    prefix_kv = prefix.reshape(-1, kv_heads, 2, HD).astype(jnp.float32)
    prefix_scores = jnp.einsum("nkgd,mkd->kgnm", grouped, prefix_kv[:, :, 0]) * scaling
    prefix_max = jnp.max(prefix_scores, axis=-1)
    prefix_exp = jnp.exp(prefix_scores - prefix_max[..., None])
    prefix_total = jnp.sum(prefix_exp, axis=-1)
    prefix_out = jnp.einsum("kgnm,mkd->kgnd", rounded(prefix_exp), prefix_kv[:, :, 1])
    query_resp = query_rows.reshape(resp_count, resp_len, kv_heads, GQA, HD).astype(jnp.float32)
    resp_kv = cache_resp.reshape(resp_count, resp_len, kv_heads, 2, HD).astype(jnp.float32)
    resp_scores = jnp.einsum("rnkgd,rmkd->rkgnm", query_resp, resp_kv[:, :, :, 0]) * scaling
    positions = jnp.arange(resp_len)
    causal = positions[:, None] >= positions[None, :]
    resp_scores = jnp.where(causal, resp_scores, NEG_FILL)
    resp_max = jnp.max(resp_scores, axis=-1)
    resp_exp = jnp.exp(resp_scores - resp_max[..., None])
    resp_total = jnp.sum(resp_exp, axis=-1)
    resp_out = jnp.einsum("rkgnm,rmkd->rkgnd", rounded(resp_exp), resp_kv[:, :, :, 1])
    resp_max = resp_max.transpose(1, 2, 0, 3).reshape(kv_heads, GQA, total_rows)
    resp_total = resp_total.transpose(1, 2, 0, 3).reshape(kv_heads, GQA, total_rows)
    resp_out = resp_out.transpose(1, 2, 0, 3, 4).reshape(kv_heads, GQA, total_rows, HD)
    joint_max = jnp.maximum(prefix_max, resp_max)
    prefix_factor = jnp.exp(prefix_max - joint_max)
    resp_factor = jnp.exp(resp_max - joint_max)
    merged = (prefix_out * prefix_factor[..., None] + resp_out * resp_factor[..., None]) / (
        prefix_total * prefix_factor + resp_total * resp_factor)[..., None]
    return merged.transpose(2, 0, 1, 3).reshape(total_rows, kv_heads * GQA * HD).astype(jnp.bfloat16)


def reference(queries, responses, cache_pool, page_table, lengths, routes, student_rows, projection):
    prompts = queries.shape[0]
    resp_count = queries.shape[1]
    resp_len = queries.shape[2]
    width = queries.shape[3]
    pools = cache_pool.reshape(prompts, POOL_PAGES, PAGE, cache_pool.shape[-1])

    def one_prompt(items):
        query_rows, cache_resp, pool_pages, table_row = items
        prefix = jnp.take(pool_pages, table_row.astype(jnp.int32), axis=0).reshape(-1, pool_pages.shape[-1])
        return attention(query_rows, cache_resp, prefix)

    tap = lax.map(one_prompt, (queries, responses, pools, page_table))
    tap = tap.reshape(prompts, resp_count, resp_len, width)
    live = (jnp.arange(resp_len)[None, None, :] < lengths[:, :, None]).astype(jnp.float32)
    target = routes[:, :, 0].astype(jnp.int32)
    hit_table = (target[:, :, None] == jnp.arange(prompts)[None, None, :]).astype(jnp.int32)
    earlier = jnp.cumsum(hit_table, axis=1) - hit_table
    slot_rank = jnp.sum(earlier * hit_table, axis=2)
    slot_index = (jnp.arange(prompts)[:, None] * MOST + slot_rank).astype(jnp.int32)
    slot_total = prompts * MOST
    tap_student = jnp.zeros((prompts, slot_total, resp_len, width), jnp.bfloat16)
    tap_student = tap_student.at[target, slot_index].set(tap)
    live_student = jnp.zeros((prompts, slot_total, resp_len), jnp.float32)
    live_student = live_student.at[target, slot_index].set(live)

    def add_group(summed, items):
        group_rows, group_tap, group_live = items
        flat_rows = group_rows.reshape(-1, DS)
        flat_live = group_live.reshape(-1)
        token_count = jnp.sum(flat_live)
        predicted = jnp.dot(flat_rows, projection, preferred_element_type=jnp.float32)
        weight = flat_live * (1.0 / token_count)
        grad_pred = ((predicted - group_tap.reshape(-1, width).astype(jnp.float32)) * weight[:, None]).astype(jnp.bfloat16)
        partial_value = jnp.dot(flat_rows.T, grad_pred, preferred_element_type=jnp.float32)
        return summed + rounded(partial_value), None

    start = jnp.zeros((DS, width), jnp.float32)
    summed, unused = lax.scan(add_group, start, (student_rows, tap_student, live_student))
    return summed.astype(jnp.bfloat16)
```

```python
import functools

import jax
import jax.numpy as jnp
from jax import lax
from jax.experimental import pallas as pl
from jax.experimental.pallas import tpu as pltpu
from jax.sharding import PartitionSpec as P

HD = 192
MOST = 2
GQA = 6
PAGE = 64
LMAX = 16
LOG2E = 1.4426950408889634
BF = jnp.bfloat16
F32 = jnp.float32

GRID = [(z, y, c) for z in range(2) for y in range(4) for c in range(2)]
TPGRID = [(h, x) for h in range(2) for x in range(4)]


def grp_at(z, y, c):
    return z * 8 + (y % 4) * 2 + c


def y_shift(step):
    return [(grp_at(z, y, c), grp_at(z, y + step, c)) for z, y, c in GRID]


Z_SWAP = [(grp_at(z, y, c), grp_at(1 - z, y, c)) for z, y, c in GRID]
C_SWAP = [(grp_at(z, y, c), grp_at(z, y, 1 - c)) for z, y, c in GRID]
H_SWAP = [(h * 4 + x, (1 - h) * 4 + x) for h, x in TPGRID]


def x_shift(step):
    return [(h * 4 + x, h * 4 + (x + step) % 4) for h, x in TPGRID]


def attention_kernel(table, q_ref, resp_ref, pool_ref, out_ref, kv, kt, vx, acc, sem, *, chunk):
    pages = table.shape[0]
    keys = pages * PAGE

    @pl.when(pl.program_id(0) == 0)
    def _():
        for j in range(pages):
            pltpu.make_async_copy(
                pool_ref.at[table[j]], kv.at[pl.ds(j * PAGE, PAGE)], sem.at[j * PAGE // chunk]
            ).start()

        def prepare(lo, n, rows):
            kt[:, lo : lo + n] = rows[:, 0:256].T
            values = rows[:, 128:384]
            lane = lax.broadcasted_iota(jnp.int32, values.shape, 1)
            ones = jnp.where(lane == 0, 1.0, 0.0).astype(BF)
            vx[lo : lo + n, :] = jnp.where(lane < 64, ones, values)

        prepare(keys, resp_ref.shape[0], resp_ref[...])
        for b in range(keys // chunk):
            block = kv.at[pl.ds(b * chunk, chunk)]
            pltpu.make_async_copy(block, block, sem.at[b]).wait()
            prepare(b * chunk, chunk, kv[b * chunk : (b + 1) * chunk, :])

    q = q_ref[...]
    n = q.shape[0]
    pad = jnp.zeros((n, 256 - HD), BF)
    q2 = jnp.concatenate(
        [jnp.concatenate([q[:, :HD], pad], 1), jnp.concatenate([q[:, HD:], pad], 1)], 0
    )
    scale = LOG2E * float(HD) ** -0.5
    bounds = [(keys, keys + n)] + [(b * chunk, (b + 1) * chunk) for b in range(keys // chunk)]
    top = None
    for lo, hi in bounds:
        s = jnp.dot(q2, kt[:, lo:hi], preferred_element_type=F32)
        if top is None:
            row = lax.broadcasted_iota(jnp.int32, s.shape, 0) % n
            col = lax.broadcasted_iota(jnp.int32, s.shape, 1)
            s = jnp.where((row // LMAX == col // LMAX) & (col <= row), s, -1e30)
        here = jnp.max(s, axis=1, keepdims=True) * scale
        new = here if top is None else jnp.maximum(top, here)
        p = jnp.exp2(s * scale - new).astype(BF)
        o = jnp.dot(p, vx[lo:hi, :], preferred_element_type=F32)
        acc[...] = o if top is None else acc[...] * jnp.exp2(top - new) + o
        top = new
    total = acc[...]
    ratio = total[:, 64:] / total[:, 0:1]
    out_ref[...] = jnp.concatenate([ratio[:n], ratio[n:]], 1).astype(BF)


def attention(q, resp, pool, table, chunk=512):
    n = q.shape[0]
    keys = table.shape[0] * PAGE
    pairs = q.shape[1] // (2 * HD)
    return pl.pallas_call(
        functools.partial(attention_kernel, chunk=chunk),
        grid_spec=pltpu.PrefetchScalarGridSpec(
            num_scalar_prefetch=1,
            grid=(pairs,),
            in_specs=[
                pl.BlockSpec((n, 2 * HD), lambda i, t: (0, i)),
                pl.BlockSpec(resp.shape, lambda i, t: (0, 0)),
                pl.BlockSpec(memory_space=pl.ANY),
            ],
            out_specs=pl.BlockSpec((n, 2 * HD), lambda i, t: (0, i)),
            scratch_shapes=[
                pltpu.VMEM((keys, 2 * HD), BF),
                pltpu.VMEM((256, keys + n), BF),
                pltpu.VMEM((keys + n, 256), BF),
                pltpu.VMEM((2 * n, 256), F32),
                pltpu.SemaphoreType.DMA((keys // chunk,)),
            ],
        ),
        out_shape=jax.ShapeDtypeStruct(q.shape, BF),
        compiler_params=pltpu.CompilerParams(vmem_limit_bytes=48 * 2**20),
        cost_estimate=pl.CostEstimate(
            flops=4 * GQA * n * (keys + n) * 256,
            bytes_accessed=8 * 2**20,
            transcendentals=GQA * n * (keys + n),
        ),
        name="attention",
    )(table, q, resp, pool)


def predict_kernel(x_ref, p_ref, out_ref, acc):
    k = pl.program_id(0)
    part = jnp.dot(x_ref[...], p_ref[...], preferred_element_type=F32)

    @pl.when(k == 0)
    def _():
        acc[...] = part

    @pl.when(k > 0)
    def _():
        acc[...] += part

    @pl.when(k == pl.num_programs(0) - 1)
    def _():
        out_ref[...] = acc[...].astype(BF)


def predict(x, p, block=768):
    n, k = x.shape
    m = p.shape[1]
    return pl.pallas_call(
        predict_kernel,
        grid=(k // block,),
        in_specs=[
            pl.BlockSpec((n, block), lambda i: (0, i)),
            pl.BlockSpec((block, m), lambda i: (i, 0)),
        ],
        out_specs=pl.BlockSpec((n, m), lambda i: (0, 0)),
        out_shape=jax.ShapeDtypeStruct((n, m), BF),
        scratch_shapes=[pltpu.VMEM((n, m), F32)],
        compiler_params=pltpu.CompilerParams(vmem_limit_bytes=32 * 2**20),
        cost_estimate=pl.CostEstimate(
            flops=2 * n * m * k, bytes_accessed=2 * (n * k + k * m + n * m), transcendentals=0
        ),
        name="predict",
    )(x, p)


def pick_kernel(place, x_ref, out_ref, sem):
    x, h = place[0], place[1]
    copies = []
    for z, y, c in GRID:
        prompt = z * 8 + x * 2 + c
        cf = c ^ (1 - h)
        for i, zf in enumerate((1 - z, z)):
            col = pl.multiple_of((zf * 8 + y * 2 + cf) * 384, 384)
            row = pl.multiple_of(prompt * 32, 32)
            copies.append(
                pltpu.make_async_copy(
                    x_ref.at[pl.ds(row, 32), pl.ds(col, 384)],
                    out_ref.at[pl.ds(grp_at(z, y, c) * 32, 32), pl.ds(i * 384, 384)],
                    sem,
                )
            )
            copies[-1].start()
    pltpu.make_async_copy(out_ref, out_ref, sem).wait()


def pick(x, place):
    return pl.pallas_call(
        pick_kernel,
        grid_spec=pltpu.PrefetchScalarGridSpec(
            num_scalar_prefetch=1,
            grid=(),
            in_specs=[pl.BlockSpec(memory_space=pl.ANY)],
            out_specs=pl.BlockSpec(memory_space=pl.ANY),
            scratch_shapes=[pltpu.SemaphoreType.DMA(())],
        ),
        out_shape=jax.ShapeDtypeStruct((512, 768), BF),
        name="pick",
    )(place, x)


def compact_kernel(slot_ref, x_ref, out_ref):
    n = x_ref.shape[0]
    rows = lax.broadcasted_iota(jnp.int32, (n, 256), 0)
    sel = (rows == slot_ref[...]).astype(F32).astype(BF)
    out_ref[...] = lax.dot_general(
        x_ref[...], sel, (((0,), (0,)), ((), ())), preferred_element_type=F32
    ).astype(BF)


def compact(slot, x):
    return pl.pallas_call(
        compact_kernel,
        out_shape=jax.ShapeDtypeStruct((x.shape[1], 256), BF),
        cost_estimate=pl.CostEstimate(
            flops=2 * 512 * 768 * 256, bytes_accessed=2 * 2**20, transcendentals=0
        ),
        name="compact",
    )(slot, x)


def grad_kernel(slot_ref, weight_ref, y_ref, tap_ref, out_ref):
    n = y_ref.shape[0]
    cols = lax.broadcasted_iota(jnp.int32, (256, n), 1)
    sel = (cols == slot_ref[...]).astype(F32).astype(BF)
    predicted = jnp.dot(sel, y_ref[...], preferred_element_type=F32)
    out_ref[...] = ((predicted - tap_ref[...].astype(F32)) * weight_ref[...]).astype(BF)


def grad_pred(slot, weight, y, tap):
    return pl.pallas_call(
        grad_kernel,
        out_shape=jax.ShapeDtypeStruct(tap.shape, BF),
        compiler_params=pltpu.CompilerParams(vmem_limit_bytes=32 * 2**20),
        cost_estimate=pl.CostEstimate(
            flops=2 * 512 * 256 * tap.shape[1], bytes_accessed=3 * 2**20, transcendentals=0
        ),
        name="grad_pred",
    )(slot, weight, y, tap)


def outer_kernel(place, x0, xa, xb, xc, xd, g0, ga, gb, gc, gd, send_ref, keep_ref, xbuf, gbuf, sem):
    x, h, y = place[0], place[1], place[2]

    def put_x(ref, half, dx):
        at = pl.multiple_of(half * 768, 768)
        col = pl.multiple_of(((x + dx) % 4) * 256, 256)
        return pltpu.make_async_copy(ref, xbuf.at[pl.ds(at, 768), pl.ds(col, 256)], sem.at[0])

    def put_g(ref, dy, lo, n):
        at = pl.multiple_of(((y + dy) % 4) * 256 + lo, 128)
        return pltpu.make_async_copy(ref, gbuf.at[pl.ds(at, n)], sem.at[1])

    for copy in (
        put_x(x0.at[0], h, 0),
        put_x(x0.at[1], 1 - h, 0),
        put_x(xa.at[0], h, 3),
        put_x(xa.at[1], 1 - h, 3),
        put_x(xb.at[0], h, 1),
        put_x(xb.at[1], 1 - h, 1),
        put_x(xc, h, 2),
        put_x(xd, 1 - h, 2),
        put_g(g0, 0, 0, 256),
        put_g(ga, 3, 0, 256),
        put_g(gb, 1, 0, 256),
        put_g(gc, 2, 0, 128),
        put_g(gd, 2, 128, 128),
    ):
        copy.start()
    pltpu.make_async_copy(xbuf, xbuf, sem.at[0]).wait()
    pltpu.make_async_copy(gbuf, gbuf, sem.at[1]).wait()
    for col in range(0, gbuf.shape[1], 384):
        g = gbuf[:, col : col + 384]
        send_ref[:, col : col + 384] = jnp.dot(
            xbuf[:768, :], g, preferred_element_type=F32
        ).astype(BF)
        keep_ref[:, col : col + 384] = jnp.dot(xbuf[768:, :], g, preferred_element_type=F32)


def outer(place, xs, gs):
    m = gs[0].shape[1]
    return pl.pallas_call(
        outer_kernel,
        grid_spec=pltpu.PrefetchScalarGridSpec(
            num_scalar_prefetch=1,
            grid=(),
            in_specs=[pl.BlockSpec(memory_space=pl.ANY)] * 10,
            out_specs=[pl.BlockSpec(memory_space=pltpu.VMEM)] * 2,
            scratch_shapes=[
                pltpu.VMEM((1536, 1024), BF),
                pltpu.VMEM((1024, m), BF),
                pltpu.SemaphoreType.DMA((2,)),
            ],
        ),
        out_shape=[jax.ShapeDtypeStruct((768, m), BF), jax.ShapeDtypeStruct((768, m), F32)],
        compiler_params=pltpu.CompilerParams(vmem_limit_bytes=32 * 2**20),
        cost_estimate=pl.CostEstimate(
            flops=2 * 1536 * 1024 * m, bytes_accessed=12 * 2**20, transcendentals=0
        ),
        name="outer",
    )(place, *xs, *gs)


def slot_rows(route):
    same = route[:, None] == route[None, :]
    earlier = jnp.arange(16)[None, :] < jnp.arange(16)[:, None]
    rank = jnp.sum((same & earlier).astype(jnp.int32), axis=1)
    rows = (route * (MOST * LMAX) + rank * LMAX)[:, None] + jnp.arange(LMAX)[None, :]
    return rows.reshape(-1)


def body(queries, responses, cache_pool, page_table, lengths, routes, student_rows, projection):
    gi = lax.axis_index("grp")
    ti = lax.axis_index("tp")
    z, y, c = gi // 8, (gi // 2) % 4, gi % 2
    h, x = ti // 4, ti % 4
    place = jnp.stack([x, h, y]).astype(jnp.int32)
    route = routes[0, :, 0]
    all_routes = lax.all_gather(route, "grp", tiled=True)

    rows = student_rows[0].reshape(-1, student_rows.shape[-1])
    share = pick(rows, place)
    share = lax.all_to_all(share, "grp", split_axis=0, concat_axis=0, tiled=True)

    predicted = predict(rows, projection)
    predicted = lax.all_to_all(predicted, "grp", split_axis=0, concat_axis=0, tiled=True)

    tap = attention(
        queries[0].reshape(256, -1), responses[0].reshape(256, -1), cache_pool, page_table[0]
    )

    shared_prompt = z * 8 + x * 2 + c
    shared_route = lax.dynamic_slice_in_dim(all_routes, shared_prompt * 16, 16)
    mine = compact(slot_rows(shared_route)[None, :], share)
    other = lax.ppermute(mine, "tp", H_SWAP)
    x0 = jnp.stack([mine, other])
    xa = lax.ppermute(x0, "tp", x_shift(1))
    xb = lax.ppermute(x0, "tp", x_shift(-1))
    xc = lax.ppermute(xa[0], "tp", x_shift(1))
    xd = lax.ppermute(xb[1], "tp", x_shift(-1))

    my_lengths = lax.dynamic_index_in_dim(lengths, gi, 0, keepdims=False)
    hits = (route[:, None] == all_routes[None, :]).astype(F32)
    count = jnp.sum(hits * lengths.reshape(1, -1).astype(F32), axis=1)
    live = (jnp.arange(LMAX)[None, :] < my_lengths[:, None]).astype(F32)
    weight = (live * (1.0 / count)[:, None]).reshape(-1, 1)
    g0 = grad_pred(slot_rows(route)[:, None], weight, predicted, tap)
    ga = lax.ppermute(g0, "grp", y_shift(1))
    gb = lax.ppermute(g0, "grp", y_shift(-1))
    gc = lax.ppermute(ga[:128], "grp", y_shift(1))
    gd = lax.ppermute(gb[128:], "grp", y_shift(-1))

    send, keep = outer(place, (x0, xa, xb, xc, xd), (g0, ga, gb, gc, gd))
    total = keep + lax.ppermute(send, "grp", C_SWAP).astype(F32)
    got = lax.ppermute(total[:384].astype(BF), "grp", Z_SWAP)
    return (total[384:] + got.astype(F32)).astype(BF)


def solution(mesh):
    return jax.shard_map(
        body,
        mesh=mesh,
        in_specs=(
            P("grp", None, None, "tp"),
            P("grp", None, None, "tp"),
            P("grp", None, "tp"),
            P("grp", None),
            P(),
            P("grp", None, None),
            P("grp", None, None, None),
            P(None, "tp"),
        ),
        out_specs=P("grp", "tp"),
        check_vma=False,
    )
```

```python
import functools

import jax
import jax.numpy as jnp
from jax import lax
from jax.experimental import pallas as pl
from jax.experimental.pallas import tpu as pltpu
from jax.sharding import PartitionSpec as P

HD = 192
MOST = 2
GQA = 6
PAGE = 64
LMAX = 16
LOG2E = 1.4426950408889634
BF = jnp.bfloat16
F32 = jnp.float32
ROUTE, LENGTH = 8, 24
MIB = 2**20

GRID = [(z, y, c) for z in range(2) for y in range(4) for c in range(2)]
TPGRID = [(h, x) for h in range(2) for x in range(4)]


def grp_at(z, y, c):
    return z * 8 + (y % 4) * 2 + c


def y_shift(step):
    return [(grp_at(z, y, c), grp_at(z, y + step, c)) for z, y, c in GRID]


Z_SWAP = [(grp_at(z, y, c), grp_at(1 - z, y, c)) for z, y, c in GRID]
C_SWAP = [(grp_at(z, y, c), grp_at(z, y, 1 - c)) for z, y, c in GRID]
H_SWAP = [(h * 4 + x, (1 - h) * 4 + x) for h, x in TPGRID]


def x_shift(step):
    return [(h * 4 + x, h * 4 + (x + step) % 4) for h, x in TPGRID]


def attention_kernel(table, q_ref, resp_ref, pool_ref, out_ref, kv, q2, acc, tops, *, chunk, mb):
    pages = table.shape[0]
    n = q_ref.shape[0]
    heads = q_ref.shape[1] // HD
    scale = LOG2E * float(HD) ** -0.5
    pad = jnp.zeros((n, 256 - HD), BF)
    for i in range(heads):
        q2[i * n : (i + 1) * n, :] = jnp.concatenate([q_ref[:, i * HD : (i + 1) * HD], pad], 1)

    def fold(rows, first):
        kt = rows[:, 0:256].T
        values = rows[:, 128:384]
        lane = lax.broadcasted_iota(jnp.int32, values.shape, 1)
        vx = jnp.where(lane < 64, jnp.where(lane == 0, 1.0, 0.0).astype(BF), values)
        for lo in range(0, heads * n, mb):
            here = slice(lo, lo + mb)
            s = jnp.dot(q2[here, :], kt, preferred_element_type=F32)
            if first:
                row = lax.broadcasted_iota(jnp.int32, s.shape, 0) % n
                col = lax.broadcasted_iota(jnp.int32, s.shape, 1)
                s = jnp.where((row // LMAX == col // LMAX) & (col <= row), s, -1e30)
            new = jnp.max(s, axis=1, keepdims=True) * scale
            if not first:
                old = tops[here, 0:1]
                new = jnp.maximum(old, new)
            p = jnp.exp2(s * scale - new).astype(BF)
            o = jnp.dot(p, vx, preferred_element_type=F32)
            acc[here, :] = o if first else acc[here, :] * jnp.exp2(old - new) + o
            tops[here, :] = jnp.broadcast_to(new, (mb, 128))

    fold(resp_ref[...], True)
    for lo in range(0, pages * PAGE, chunk):
        for j in range(lo // PAGE, (lo + chunk) // PAGE):
            kv[j * PAGE : (j + 1) * PAGE, :] = pool_ref[table[j]]
        fold(kv[lo : lo + chunk, :], False)
    for i in range(0, heads, 2):
        ratios = []
        for j in (i, i + 1):
            total = acc[j * n : (j + 1) * n, :]
            ratios.append(total[:, 64:] / total[:, 0:1])
        out_ref[:, i * HD : (i + 2) * HD] = jnp.concatenate(ratios, 1).astype(BF)


def attention(q, resp, pool, table, chunk=2048, mb=256):
    n, width = q.shape
    keys = table.shape[0] * PAGE
    heads = width // HD
    return pl.pallas_call(
        functools.partial(attention_kernel, chunk=chunk, mb=mb),
        grid_spec=pltpu.PrefetchScalarGridSpec(
            num_scalar_prefetch=1,
            grid=(),
            in_specs=[pl.BlockSpec(memory_space=pltpu.VMEM)] * 3,
            out_specs=pl.BlockSpec(memory_space=pltpu.VMEM),
            scratch_shapes=[
                pltpu.VMEM((keys, 2 * HD), BF),
                pltpu.VMEM((heads * n, 256), BF),
                pltpu.VMEM((heads * n, 256), F32),
                pltpu.VMEM((heads * n, 128), F32),
            ],
        ),
        out_shape=jax.ShapeDtypeStruct((n, width), BF),
        compiler_params=pltpu.CompilerParams(vmem_limit_bytes=24 * MIB),
        cost_estimate=pl.CostEstimate(
            flops=4 * heads * n * (keys + n) * 256,
            bytes_accessed=8 * 2**20,
            transcendentals=heads * n * (keys + n),
        ),
        name="attention",
    )(table, q, resp, pool)


def predict_kernel(x_ref, p_ref, out_ref, acc):
    k = pl.program_id(0)
    part = jnp.dot(x_ref[...], p_ref[...], preferred_element_type=F32)

    @pl.when(k == 0)
    def _():
        acc[...] = part

    @pl.when(k > 0)
    def _():
        acc[...] += part

    @pl.when(k == pl.num_programs(0) - 1)
    def _():
        out_ref[...] = acc[...].astype(BF)


def predict(x, p, block=1536):
    n, k = x.shape
    m = p.shape[1]
    return pl.pallas_call(
        predict_kernel,
        grid=(k // block,),
        in_specs=[
            pl.BlockSpec((n, block), lambda i: (0, i)),
            pl.BlockSpec((block, m), lambda i: (i, 0)),
        ],
        out_specs=pl.BlockSpec((n, m), lambda i: (0, 0)),
        out_shape=jax.ShapeDtypeStruct((n, m), BF),
        scratch_shapes=[pltpu.VMEM((n, m), F32)],
        compiler_params=pltpu.CompilerParams(vmem_limit_bytes=52 * MIB),
        cost_estimate=pl.CostEstimate(
            flops=2 * n * m * k, bytes_accessed=2 * (n * k + k * m + n * m), transcendentals=0
        ),
        name="predict",
    )(x, p)


def pick_kernel(info, x_hbm, out_ref, x_ref, sem):
    x, h = info[0], info[1]
    for z, c in ((0, 0), (0, 1), (1, 0), (1, 1)):
        row = pl.multiple_of((z * 8 + x * 2 + c) * 32, 32)
        there = x_ref.at[pl.ds((z * 2 + c) * 32, 32)]
        pltpu.make_async_copy(x_hbm.at[pl.ds(row, 32)], there, sem).start()
    token = lax.broadcasted_iota(jnp.int32, (32, 128), 0) * 128
    token += lax.broadcasted_iota(jnp.int32, (32, 128), 1)
    mark = jnp.full((32, 128), 127, jnp.int32)
    for r in range(16):
        route = info[ROUTE + r]
        rank = jnp.int32(0)
        for earlier in range(r):
            rank += (info[ROUTE + earlier] == route).astype(jnp.int32)
        dead = jnp.where(token % LMAX < info[LENGTH + r], 0, 64)
        mark = jnp.where(token // LMAX == r, route * MOST + rank + dead, mark)
    mark = mark.astype(F32).astype(BF)
    pltpu.make_async_copy(x_ref, x_ref, sem).wait()

    for z, y, c in GRID:
        at = grp_at(z, y, c) * 32
        row = (z * 2 + c) * 32
        for i, zf in enumerate((1 - z, z)):
            block = zf * 8 + y * 2 + jnp.where(h == 0, 1 - c, c)
            col = pl.multiple_of(block * 384, 384)
            out_ref[at : at + 32, i * 384 : (i + 1) * 384] = x_ref[row : row + 32, pl.ds(col, 384)]
        out_ref[at : at + 32, 768:] = mark


def pick(info, x):
    return pl.pallas_call(
        pick_kernel,
        grid_spec=pltpu.PrefetchScalarGridSpec(
            num_scalar_prefetch=1,
            grid=(),
            in_specs=[pl.BlockSpec(memory_space=pl.ANY)],
            out_specs=pl.BlockSpec(memory_space=pltpu.VMEM),
            scratch_shapes=[pltpu.VMEM((128, x.shape[1]), BF), pltpu.SemaphoreType.DMA(())],
        ),
        out_shape=jax.ShapeDtypeStruct((512, 896), BF),
        compiler_params=pltpu.CompilerParams(vmem_limit_bytes=58 * MIB),
        cost_estimate=pl.CostEstimate(flops=0, bytes_accessed=3 * 2**20, transcendentals=0),
        name="pick",
    )(info, x)


def slot_of(mark):
    lane = lax.broadcasted_iota(jnp.int32, mark.shape, 1)
    return jnp.where(mark < 64, mark, mark - 64) * LMAX + lane % LMAX


def compact_kernel(info, x_ref, out_ref, meta_ref):
    def marks_of(prompt):
        at = pl.multiple_of(prompt * 32, 32)
        rows = x_ref[pl.ds(at, 32), 768:].astype(F32)
        return jnp.concatenate([rows[0:1], rows[1:2]], 1).astype(jnp.int32)

    slot = slot_of(marks_of(info[3]))
    rows = lax.broadcasted_iota(jnp.int32, (512, 256), 0)
    sel = (rows == slot).astype(F32).astype(BF)
    out_ref[...] = lax.dot_general(
        x_ref[:, :768], sel, (((0,), (0,)), ((), ())), preferred_element_type=F32
    ).astype(BF)

    every = x_ref[:, 768:].astype(F32)
    own = marks_of(info[4])
    weight = jnp.zeros(own.shape, F32)
    for s in range(16):
        hit = (every == 2.0 * s) | (every == 2.0 * s + 1.0)
        count = jnp.sum(jnp.sum(hit.astype(F32), axis=0, keepdims=True), axis=1, keepdims=True)
        weight = jnp.where((own == 2 * s) | (own == 2 * s + 1), 1.0 / count, weight)
    meta_ref[...] = jnp.concatenate(
        [slot_of(own).astype(F32), weight, jnp.zeros((6, 256), F32)], 0
    )


def compact(info, x):
    return pl.pallas_call(
        compact_kernel,
        grid_spec=pltpu.PrefetchScalarGridSpec(
            num_scalar_prefetch=1,
            grid=(),
            in_specs=[pl.BlockSpec(memory_space=pltpu.VMEM)],
            out_specs=[pl.BlockSpec(memory_space=pltpu.VMEM)] * 2,
        ),
        out_shape=[
            jax.ShapeDtypeStruct((768, 256), BF),
            jax.ShapeDtypeStruct((8, 256), F32),
        ],
        compiler_params=pltpu.CompilerParams(vmem_limit_bytes=12 * MIB),
        cost_estimate=pl.CostEstimate(
            flops=2 * 512 * 768 * 256, bytes_accessed=2 * 2**20, transcendentals=0
        ),
        name="compact",
    )(info, x)


def grad_kernel(meta_ref, y_ref, tap_ref, out_ref):
    n = y_ref.shape[0]
    meta = meta_ref[...].T
    cols = lax.broadcasted_iota(jnp.int32, (256, n), 1)
    sel = (cols == meta[:, 0:1].astype(jnp.int32)).astype(F32).astype(BF)
    predicted = jnp.dot(sel, y_ref[...], preferred_element_type=F32)
    out_ref[...] = ((predicted - tap_ref[...].astype(F32)) * meta[:, 1:2]).astype(BF)


def grad_pred(meta, y, tap):
    return pl.pallas_call(
        grad_kernel,
        in_specs=[pl.BlockSpec(memory_space=pltpu.VMEM)] * 3,
        out_specs=pl.BlockSpec(memory_space=pltpu.VMEM),
        out_shape=jax.ShapeDtypeStruct(tap.shape, BF),
        compiler_params=pltpu.CompilerParams(vmem_limit_bytes=16 * MIB),
        cost_estimate=pl.CostEstimate(
            flops=2 * 512 * 256 * tap.shape[1], bytes_accessed=3 * 2**20, transcendentals=0
        ),
        name="grad_pred",
    )(meta, y, tap)


def send_kernel(info, *refs):
    xs, gs, (out_ref, keep_ref, gbuf_ref, xbuf) = refs[:8], refs[8:13], refs[13:]
    x, h, y = info[0], info[1], info[2]
    for ref, dy, lo in zip(gs, (0, 1, 3, 2, 2), (0, 0, 0, 0, 128)):
        at = pl.multiple_of(((y + dy + 4 - x) % 4) * 256 + lo, 128)
        gbuf_ref[pl.ds(at, ref.shape[0]), :] = ref[...]
    for i in range(4):
        here = slice(i * 256, (i + 1) * 256)

        @pl.when(h == 0)
        def _():
            xbuf[:, here] = xs[i][...]
            keep_ref[:, here] = xs[4 + i][...]

        @pl.when(h == 1)
        def _():
            xbuf[:, here] = xs[4 + i][...]
            keep_ref[:, here] = xs[i][...]

    out_ref[...] = jnp.dot(xbuf[...], gbuf_ref[...], preferred_element_type=F32).astype(BF)


def outer_send(info, xs, gs):
    m = gs[0].shape[1]
    return pl.pallas_call(
        send_kernel,
        grid_spec=pltpu.PrefetchScalarGridSpec(
            num_scalar_prefetch=1,
            grid=(),
            in_specs=[pl.BlockSpec(memory_space=pltpu.VMEM)] * 13,
            out_specs=[pl.BlockSpec(memory_space=pltpu.VMEM)] * 3,
            scratch_shapes=[pltpu.VMEM((768, 1024), BF)],
        ),
        out_shape=[
            jax.ShapeDtypeStruct((768, m), BF),
            jax.ShapeDtypeStruct((768, 1024), BF),
            jax.ShapeDtypeStruct((1024, m), BF),
        ],
        compiler_params=pltpu.CompilerParams(vmem_limit_bytes=16 * MIB),
        cost_estimate=pl.CostEstimate(
            flops=2 * 768 * 1024 * m, bytes_accessed=8 * 2**20, transcendentals=0
        ),
        name="outer_send",
    )(info, *xs, *gs)


def keep_kernel(x_ref, g_ref, out_ref, *, lo):
    rows = out_ref.shape[0]
    out_ref[...] = jnp.dot(x_ref[lo : lo + rows, :], g_ref[...], preferred_element_type=F32)


def outer_keep(x, g, lo):
    m = g.shape[1]
    return pl.pallas_call(
        functools.partial(keep_kernel, lo=lo),
        in_specs=[pl.BlockSpec(memory_space=pltpu.VMEM)] * 2,
        out_specs=pl.BlockSpec(memory_space=pltpu.VMEM),
        out_shape=jax.ShapeDtypeStruct((384, m), F32),
        compiler_params=pltpu.CompilerParams(vmem_limit_bytes=16 * MIB),
        cost_estimate=pl.CostEstimate(
            flops=2 * 384 * 1024 * m, bytes_accessed=4 * 2**20, transcendentals=0
        ),
        name="outer_keep",
    )(x, g)


def body(queries, responses, cache_pool, page_table, lengths, routes, student_rows, projection):
    gi = lax.axis_index("grp")
    ti = lax.axis_index("tp")
    z, y, c = gi // 8, (gi // 2) % 4, gi % 2
    h, x = ti // 4, ti % 4
    my_lengths = lax.dynamic_index_in_dim(lengths, gi, 0, keepdims=False)
    own = jnp.stack([x, h, y, z * 8 + x * 2 + c, gi, gi, gi, gi]).astype(jnp.int32)
    info = jnp.concatenate([own, routes[0, :, 0], my_lengths])

    rows = student_rows[0].reshape(-1, student_rows.shape[-1])
    share = pick(info, rows)
    share = lax.all_to_all(share, "grp", split_axis=0, concat_axis=0, tiled=True)

    predicted = predict(rows, projection)
    mine, meta = compact(info, share)
    predicted, mine = lax.optimization_barrier((predicted, mine))
    predicted = lax.all_to_all(predicted, "grp", split_axis=0, concat_axis=0, tiled=True)

    other = lax.ppermute(mine, "tp", H_SWAP)
    ma = lax.ppermute(mine, "tp", x_shift(1))
    mb = lax.ppermute(mine, "tp", x_shift(-1))

    q = queries[0].reshape(256, -1)
    q, meta = lax.optimization_barrier((q, meta))
    tap = attention(q, responses[0].reshape(256, -1), cache_pool, page_table[0])
    other, ma, mb, tap = lax.optimization_barrier((other, ma, mb, tap))
    oa = lax.ppermute(other, "tp", x_shift(1))
    ob = lax.ppermute(other, "tp", x_shift(-1))
    mc = lax.ppermute(ma, "tp", x_shift(1))

    g = grad_pred(meta, predicted, tap)
    ga = lax.ppermute(g, "grp", y_shift(1))
    gb = lax.ppermute(g, "grp", y_shift(-1))
    ga, gb, ob = lax.optimization_barrier((ga, gb, ob))
    gc = lax.ppermute(ga[:128], "grp", y_shift(1))
    gd = lax.ppermute(gb[128:], "grp", y_shift(-1))
    oc = lax.ppermute(ob, "tp", x_shift(-1))
    xs = (mine, mb, mc, ma, other, ob, oc, oa)

    send, kept, grads = outer_send(info, xs, (g, gb, ga, gc, gd))
    got = lax.ppermute(send, "grp", C_SWAP)
    to_z = outer_keep(kept, grads, 0) + got[:384].astype(F32)
    to_z = to_z.astype(BF)
    kept, to_z = lax.optimization_barrier((kept, to_z))
    stay = outer_keep(kept, grads, 384) + got[384:].astype(F32)
    return (stay + lax.ppermute(to_z, "grp", Z_SWAP).astype(F32)).astype(BF)


def solution(mesh):
    return jax.shard_map(
        body,
        mesh=mesh,
        in_specs=(
            P("grp", None, None, "tp"),
            P("grp", None, None, "tp"),
            P("grp", None, "tp"),
            P("grp", None),
            P(),
            P("grp", None, None),
            P("grp", None, None, None),
            P(None, "tp"),
        ),
        out_specs=P("grp", "tp"),
        check_vma=False,
    )
```

```python
import functools

import jax
import jax.numpy as jnp
from jax import lax
from jax.experimental import pallas as pl
from jax.experimental.pallas import tpu as pltpu
from jax.sharding import PartitionSpec as P

HD = 192
MOST = 2
GQA = 6
PAGE = 64
LMAX = 16
LOG2E = 1.4426950408889634
BF = jnp.bfloat16
F32 = jnp.float32
MIB = 2**20

GRID = [(z, y, c) for z in range(2) for y in range(4) for c in range(2)]
TPGRID = [(h, x) for h in range(2) for x in range(4)]


def grp_at(z, y, c):
    return z * 8 + (y % 4) * 2 + c


def y_shift(step):
    return [(grp_at(z, y, c), grp_at(z, y + step, c)) for z, y, c in GRID]


Z_SWAP = [(grp_at(z, y, c), grp_at(1 - z, y, c)) for z, y, c in GRID]
C_SWAP = [(grp_at(z, y, c), grp_at(z, y, 1 - c)) for z, y, c in GRID]
H_SWAP = [(h * 4 + x, (1 - h) * 4 + x) for h, x in TPGRID]


def x_shift(step):
    return [(h * 4 + x, h * 4 + (x + step) % 4) for h, x in TPGRID]


def coordinates():
    g, t = lax.axis_index("grp"), lax.axis_index("tp")
    return g // 8, (g // 2) % 4, g % 2, t // 4, t % 4


def attention_kernel(table, q_ref, resp_ref, pool_ref, out_ref, kv, q2, acc, tops, *, chunk, mb):
    pages = table.shape[0]
    n = q_ref.shape[0]
    heads = q_ref.shape[1] // HD
    scale = LOG2E * float(HD) ** -0.5
    pad = jnp.zeros((n, 256 - HD), BF)
    for i in range(heads):
        q2[i * n : (i + 1) * n, :] = jnp.concatenate([q_ref[:, i * HD : (i + 1) * HD], pad], 1)

    def fold(rows, first):
        kt = rows[:, 0:256].T
        values = rows[:, 128:384]
        lane = lax.broadcasted_iota(jnp.int32, values.shape, 1)
        vx = jnp.where(lane < 64, jnp.where(lane == 0, 1.0, 0.0).astype(BF), values)
        for lo in range(0, heads * n, mb):
            here = slice(lo, lo + mb)
            s = jnp.dot(q2[here, :], kt, preferred_element_type=F32)
            if first:
                row = lax.broadcasted_iota(jnp.int32, s.shape, 0) % n
                col = lax.broadcasted_iota(jnp.int32, s.shape, 1)
                s = jnp.where((row // LMAX == col // LMAX) & (col <= row), s, -1e30)
            new = jnp.max(s, axis=1, keepdims=True) * scale
            if not first:
                old = tops[here, 0:1]
                new = jnp.maximum(old, new)
            p = jnp.exp2(s * scale - new).astype(BF)
            o = jnp.dot(p, vx, preferred_element_type=F32)
            acc[here, :] = o if first else acc[here, :] * jnp.exp2(old - new) + o
            tops[here, :] = jnp.broadcast_to(new, (mb, 128))

    fold(resp_ref[...], True)
    for lo in range(0, pages * PAGE, chunk):
        for j in range(lo // PAGE, (lo + chunk) // PAGE):
            kv[j * PAGE : (j + 1) * PAGE, :] = pool_ref[table[j]]
        fold(kv[lo : lo + chunk, :], False)
    for i in range(0, heads, 2):
        ratios = []
        for j in (i, i + 1):
            total = acc[j * n : (j + 1) * n, :]
            ratios.append(total[:, 64:] / total[:, 0:1])
        out_ref[:, i * HD : (i + 2) * HD] = jnp.concatenate(ratios, 1).astype(BF)


def attention(q, resp, pool, table, chunk=2048, mb=256):
    n, width = q.shape
    keys = table.shape[0] * PAGE
    heads = width // HD
    return pl.pallas_call(
        functools.partial(attention_kernel, chunk=chunk, mb=mb),
        grid_spec=pltpu.PrefetchScalarGridSpec(
            num_scalar_prefetch=1,
            grid=(),
            in_specs=[pl.BlockSpec(memory_space=pltpu.VMEM)] * 3,
            out_specs=pl.BlockSpec(memory_space=pltpu.VMEM),
            scratch_shapes=[
                pltpu.VMEM((keys, 2 * HD), BF),
                pltpu.VMEM((heads * n, 256), BF),
                pltpu.VMEM((heads * n, 256), F32),
                pltpu.VMEM((heads * n, 128), F32),
            ],
        ),
        out_shape=jax.ShapeDtypeStruct((n, width), BF),
        compiler_params=pltpu.CompilerParams(vmem_limit_bytes=24 * MIB),
        cost_estimate=pl.CostEstimate(
            flops=4 * heads * n * (keys + n) * 256,
            bytes_accessed=8 * 2**20,
            transcendentals=heads * n * (keys + n),
        ),
        name="attention",
    )(table, q, resp, pool)


def predict_kernel(x_ref, p_ref, out_ref, acc):
    k = pl.program_id(0)
    part = jnp.dot(x_ref[...], p_ref[...], preferred_element_type=F32)

    @pl.when(k == 0)
    def _():
        acc[...] = part

    @pl.when(k > 0)
    def _():
        acc[...] += part

    @pl.when(k == pl.num_programs(0) - 1)
    def _():
        out_ref[...] = acc[...].astype(BF)


def predict(x, p, block=1536):
    n, k = x.shape
    m = p.shape[1]
    return pl.pallas_call(
        predict_kernel,
        grid=(k // block,),
        in_specs=[
            pl.BlockSpec((n, block), lambda i: (0, i)),
            pl.BlockSpec((block, m), lambda i: (i, 0)),
        ],
        out_specs=pl.BlockSpec((n, m), lambda i: (0, 0)),
        out_shape=jax.ShapeDtypeStruct((n, m), BF),
        scratch_shapes=[pltpu.VMEM((n, m), F32)],
        compiler_params=pltpu.CompilerParams(vmem_limit_bytes=52 * MIB),
        cost_estimate=pl.CostEstimate(
            flops=2 * n * m * k, bytes_accessed=2 * (n * k + k * m + n * m), transcendentals=0
        ),
        name="predict",
    )(x, p)


def pick_kernel(routes, lengths, x_hbm, out_ref, x_ref, sem):
    mine = lax.axis_index("grp")
    _, _, _, h, x = coordinates()
    for z, c in ((0, 0), (0, 1), (1, 0), (1, 1)):
        row = pl.multiple_of((z * 8 + x * 2 + c) * 32, 32)
        there = x_ref.at[pl.ds((z * 2 + c) * 32, 32)]
        pltpu.make_async_copy(x_hbm.at[pl.ds(row, 32)], there, sem).start()
    token = lax.broadcasted_iota(jnp.int32, (32, 128), 0) * 128
    token += lax.broadcasted_iota(jnp.int32, (32, 128), 1)
    mark = jnp.full((32, 128), 127, jnp.int32)
    for r in range(16):
        route = routes[r]
        rank = jnp.int32(0)
        for earlier in range(r):
            rank += (routes[earlier] == route).astype(jnp.int32)
        dead = jnp.where(token % LMAX < lengths[mine, r], 0, 64)
        mark = jnp.where(token // LMAX == r, route * MOST + rank + dead, mark)
    mark = mark.astype(F32).astype(BF)
    pltpu.make_async_copy(x_ref, x_ref, sem).wait()

    for z, y, c in GRID:
        at = grp_at(z, y, c) * 32
        row = (z * 2 + c) * 32
        for i, zf in enumerate((1 - z, z)):
            block = zf * 8 + y * 2 + jnp.where(h == 0, 1 - c, c)
            col = pl.multiple_of(block * 384, 384)
            out_ref[at : at + 32, i * 384 : (i + 1) * 384] = x_ref[row : row + 32, pl.ds(col, 384)]
        out_ref[at : at + 32, 768:] = mark


def pick(routes, lengths, x):
    return pl.pallas_call(
        pick_kernel,
        grid_spec=pltpu.PrefetchScalarGridSpec(
            num_scalar_prefetch=2,
            grid=(),
            in_specs=[pl.BlockSpec(memory_space=pl.ANY)],
            out_specs=pl.BlockSpec(memory_space=pltpu.VMEM),
            scratch_shapes=[pltpu.VMEM((128, x.shape[1]), BF), pltpu.SemaphoreType.DMA(())],
        ),
        out_shape=jax.ShapeDtypeStruct((512, 896), BF),
        compiler_params=pltpu.CompilerParams(vmem_limit_bytes=58 * MIB),
        cost_estimate=pl.CostEstimate(flops=0, bytes_accessed=3 * 2**20, transcendentals=0),
        name="pick",
    )(routes, lengths, x)


def slot_of(mark):
    lane = lax.broadcasted_iota(jnp.int32, mark.shape, 1)
    return jnp.where(mark < 64, mark, mark - 64) * LMAX + lane % LMAX


def compact_kernel(x_ref, out_ref, meta_ref):
    z, _, c, _, x = coordinates()

    def marks_of(prompt):
        at = pl.multiple_of(prompt * 32, 32)
        rows = x_ref[pl.ds(at, 32), 768:].astype(F32)
        return jnp.concatenate([rows[0:1], rows[1:2]], 1).astype(jnp.int32)

    slot = slot_of(marks_of(z * 8 + x * 2 + c))
    rows = lax.broadcasted_iota(jnp.int32, (512, 256), 0)
    sel = (rows == slot).astype(F32).astype(BF)
    out_ref[...] = lax.dot_general(
        x_ref[:, :768], sel, (((0,), (0,)), ((), ())), preferred_element_type=F32
    ).astype(BF)

    every = x_ref[:, 768:].astype(F32)
    own = marks_of(lax.axis_index("grp"))
    weight = jnp.zeros(own.shape, F32)
    for s in range(16):
        hit = (every == 2.0 * s) | (every == 2.0 * s + 1.0)
        count = jnp.sum(jnp.sum(hit.astype(F32), axis=0, keepdims=True), axis=1, keepdims=True)
        weight = jnp.where((own == 2 * s) | (own == 2 * s + 1), 1.0 / count, weight)
    meta_ref[...] = jnp.concatenate(
        [slot_of(own).astype(F32), weight, jnp.zeros((6, 256), F32)], 0
    )


def compact(x):
    return pl.pallas_call(
        compact_kernel,
        in_specs=[pl.BlockSpec(memory_space=pltpu.VMEM)],
        out_specs=[pl.BlockSpec(memory_space=pltpu.VMEM)] * 2,
        out_shape=[
            jax.ShapeDtypeStruct((768, 256), BF),
            jax.ShapeDtypeStruct((8, 256), F32),
        ],
        compiler_params=pltpu.CompilerParams(vmem_limit_bytes=12 * MIB),
        cost_estimate=pl.CostEstimate(
            flops=2 * 512 * 768 * 256, bytes_accessed=2 * 2**20, transcendentals=0
        ),
        name="compact",
    )(x)


def grad_kernel(meta_ref, y_ref, tap_ref, out_ref):
    n = y_ref.shape[0]
    meta = meta_ref[...].T
    cols = lax.broadcasted_iota(jnp.int32, (256, n), 1)
    sel = (cols == meta[:, 0:1].astype(jnp.int32)).astype(F32).astype(BF)
    predicted = jnp.dot(sel, y_ref[...], preferred_element_type=F32)
    out_ref[...] = ((predicted - tap_ref[...].astype(F32)) * meta[:, 1:2]).astype(BF)


def grad_pred(meta, y, tap):
    return pl.pallas_call(
        grad_kernel,
        in_specs=[pl.BlockSpec(memory_space=pltpu.VMEM)] * 3,
        out_specs=pl.BlockSpec(memory_space=pltpu.VMEM),
        out_shape=jax.ShapeDtypeStruct(tap.shape, BF),
        compiler_params=pltpu.CompilerParams(vmem_limit_bytes=10 * MIB),
        cost_estimate=pl.CostEstimate(
            flops=2 * 512 * 256 * tap.shape[1], bytes_accessed=3 * 2**20, transcendentals=0
        ),
        name="grad_pred",
    )(meta, y, tap)


def send_kernel(*refs):
    xs, gs, (out_ref, keep_ref, gbuf_ref, xbuf) = refs[:8], refs[8:13], refs[13:]
    _, y, _, h, x = coordinates()
    for ref, dy, lo in zip(gs, (0, 1, 3, 2, 2), (0, 0, 0, 0, 128)):
        at = pl.multiple_of(((y + dy + 4 - x) % 4) * 256 + lo, 128)
        gbuf_ref[pl.ds(at, ref.shape[0]), :] = ref[...]
    for i in range(4):
        here = slice(i * 256, (i + 1) * 256)

        @pl.when(h == 0)
        def _():
            xbuf[:, here] = xs[i][...]
            keep_ref[:, here] = xs[4 + i][...]

        @pl.when(h == 1)
        def _():
            xbuf[:, here] = xs[4 + i][...]
            keep_ref[:, here] = xs[i][...]

    out_ref[...] = jnp.dot(xbuf[...], gbuf_ref[...], preferred_element_type=F32).astype(BF)


def outer_send(xs, gs):
    m = gs[0].shape[1]
    return pl.pallas_call(
        send_kernel,
        in_specs=[pl.BlockSpec(memory_space=pltpu.VMEM)] * 13,
        out_specs=[pl.BlockSpec(memory_space=pltpu.VMEM)] * 3,
        scratch_shapes=[pltpu.VMEM((768, 1024), BF)],
        out_shape=[
            jax.ShapeDtypeStruct((768, m), BF),
            jax.ShapeDtypeStruct((768, 1024), BF),
            jax.ShapeDtypeStruct((1024, m), BF),
        ],
        compiler_params=pltpu.CompilerParams(vmem_limit_bytes=10 * MIB),
        cost_estimate=pl.CostEstimate(
            flops=2 * 768 * 1024 * m, bytes_accessed=8 * 2**20, transcendentals=0
        ),
        name="outer_send",
    )(*xs, *gs)


def keep_kernel(x_ref, g_ref, out_ref, *, lo):
    rows = out_ref.shape[0]
    out_ref[...] = jnp.dot(x_ref[lo : lo + rows, :], g_ref[...], preferred_element_type=F32)


def outer_keep(x, g, lo):
    m = g.shape[1]
    return pl.pallas_call(
        functools.partial(keep_kernel, lo=lo),
        in_specs=[pl.BlockSpec(memory_space=pltpu.VMEM)] * 2,
        out_specs=pl.BlockSpec(memory_space=pltpu.VMEM),
        out_shape=jax.ShapeDtypeStruct((384, m), F32),
        compiler_params=pltpu.CompilerParams(vmem_limit_bytes=10 * MIB),
        cost_estimate=pl.CostEstimate(
            flops=2 * 384 * 1024 * m, bytes_accessed=4 * 2**20, transcendentals=0
        ),
        name="outer_keep",
    )(x, g)


def body(queries, responses, cache_pool, page_table, lengths, routes, student_rows, projection):
    rows = student_rows[0].reshape(-1, student_rows.shape[-1])
    share = pick(routes.reshape(-1), lengths, rows)
    share = lax.all_to_all(share, "grp", split_axis=0, concat_axis=0, tiled=True)

    predicted = predict(rows, projection)
    mine, meta = compact(share)
    predicted, mine = lax.optimization_barrier((predicted, mine))
    predicted = lax.all_to_all(predicted, "grp", split_axis=0, concat_axis=0, tiled=True)

    other = lax.ppermute(mine, "tp", H_SWAP)
    ma = lax.ppermute(mine, "tp", x_shift(1))
    mb = lax.ppermute(mine, "tp", x_shift(-1))
    mc = lax.ppermute(mine, "tp", x_shift(2))

    q = queries[0].reshape(256, -1)
    q, meta = lax.optimization_barrier((q, meta))
    tap = attention(q, responses[0].reshape(256, -1), cache_pool, page_table[0])
    g = grad_pred(meta, predicted, tap)
    ga = lax.ppermute(g, "grp", y_shift(1))
    gb = lax.ppermute(g, "grp", y_shift(-1))
    other, ma, mb, mc, g = lax.optimization_barrier((other, ma, mb, mc, g))
    oa = lax.ppermute(other, "tp", x_shift(1))
    ob = lax.ppermute(other, "tp", x_shift(-1))
    oc = lax.ppermute(other, "tp", x_shift(2))
    ga, gb, oa = lax.optimization_barrier((ga, gb, oa))
    gc = lax.ppermute(ga[:128], "grp", y_shift(1))
    gd = lax.ppermute(gb[128:], "grp", y_shift(-1))
    xs = (mine, mb, mc, ma, other, ob, oc, oa)

    send, kept, grads = outer_send(xs, (g, gb, ga, gc, gd))
    got = lax.ppermute(send, "grp", C_SWAP)
    to_z = outer_keep(kept, grads, 0) + got[:384].astype(F32)
    to_z = to_z.astype(BF)
    kept, to_z = lax.optimization_barrier((kept, to_z))
    stay = outer_keep(kept, grads, 384) + got[384:].astype(F32)
    return (stay + lax.ppermute(to_z, "grp", Z_SWAP).astype(F32)).astype(BF)


def solution(mesh):
    return jax.shard_map(
        body,
        mesh=mesh,
        in_specs=(
            P("grp", None, None, "tp"),
            P("grp", None, None, "tp"),
            P("grp", None, "tp"),
            P("grp", None),
            P(),
            P("grp", None, None),
            P("grp", None, None, None),
            P(None, "tp"),
        ),
        out_specs=P("grp", "tp"),
        check_vma=False,
    )
```

```python
import functools

import jax
import jax.numpy as jnp
from jax import lax
from jax.experimental import pallas as pl
from jax.experimental.pallas import tpu as pltpu
from jax.sharding import PartitionSpec as P

HD = 192
MOST = 2
GQA = 6
PAGE = 64
LMAX = 16
LOG2E = 1.4426950408889634
BF = jnp.bfloat16
F32 = jnp.float32
MIB = 2**20

GRID = [(z, y, c) for z in range(2) for y in range(4) for c in range(2)]
TPGRID = [(h, x) for h in range(2) for x in range(4)]


def grp_at(z, y, c):
    return z * 8 + (y % 4) * 2 + c


def y_shift(step):
    return [(grp_at(z, y, c), grp_at(z, y + step, c)) for z, y, c in GRID]


Z_SWAP = [(grp_at(z, y, c), grp_at(1 - z, y, c)) for z, y, c in GRID]
C_SWAP = [(grp_at(z, y, c), grp_at(z, y, 1 - c)) for z, y, c in GRID]
H_SWAP = [(h * 4 + x, (1 - h) * 4 + x) for h, x in TPGRID]


def x_shift(step):
    return [(h * 4 + x, h * 4 + (x + step) % 4) for h, x in TPGRID]


def coordinates():
    g, t = lax.axis_index("grp"), lax.axis_index("tp")
    return g // 8, (g // 2) % 4, g % 2, t // 4, t % 4


def attention_kernel(table, q_ref, resp_ref, pool_ref, out_ref, kv, q2, acc, tops, *, chunk, mb):
    pages = table.shape[0]
    n = q_ref.shape[0]
    heads = q_ref.shape[1] // HD
    scale = LOG2E * float(HD) ** -0.5
    pad = jnp.zeros((n, 256 - HD), BF)
    for i in range(heads):
        q2[i * n : (i + 1) * n, :] = jnp.concatenate([q_ref[:, i * HD : (i + 1) * HD], pad], 1)

    def fold(rows, first):
        kt = rows[:, 0:256].T
        values = rows[:, 128:384]
        lane = lax.broadcasted_iota(jnp.int32, values.shape, 1)
        vx = jnp.where(lane < 64, jnp.where(lane == 0, 1.0, 0.0).astype(BF), values)
        for lo in range(0, heads * n, mb):
            here = slice(lo, lo + mb)
            s = jnp.dot(q2[here, :], kt, preferred_element_type=F32)
            if first:
                row = lax.broadcasted_iota(jnp.int32, s.shape, 0) % n
                col = lax.broadcasted_iota(jnp.int32, s.shape, 1)
                s = jnp.where((row // LMAX == col // LMAX) & (col <= row), s, -1e30)
            new = jnp.max(s, axis=1, keepdims=True) * scale
            if not first:
                old = tops[here, 0:1]
                new = jnp.maximum(old, new)
            p = jnp.exp2(s * scale - new).astype(BF)
            o = jnp.dot(p, vx, preferred_element_type=F32)
            acc[here, :] = o if first else acc[here, :] * jnp.exp2(old - new) + o
            tops[here, :] = jnp.broadcast_to(new, (mb, 128))

    fold(resp_ref[...], True)
    for lo in range(0, pages * PAGE, chunk):
        for j in range(lo // PAGE, (lo + chunk) // PAGE):
            kv[j * PAGE : (j + 1) * PAGE, :] = pool_ref[table[j]]
        fold(kv[lo : lo + chunk, :], False)
    for i in range(0, heads, 2):
        ratios = []
        for j in (i, i + 1):
            total = acc[j * n : (j + 1) * n, :]
            ratios.append(total[:, 64:] / total[:, 0:1])
        out_ref[:, i * HD : (i + 2) * HD] = jnp.concatenate(ratios, 1).astype(BF)


def attention(q, resp, pool, table, chunk=2048, mb=256):
    n, width = q.shape
    keys = table.shape[0] * PAGE
    heads = width // HD
    return pl.pallas_call(
        functools.partial(attention_kernel, chunk=chunk, mb=mb),
        grid_spec=pltpu.PrefetchScalarGridSpec(
            num_scalar_prefetch=1,
            grid=(),
            in_specs=[pl.BlockSpec(memory_space=pltpu.VMEM)] * 3,
            out_specs=pl.BlockSpec(memory_space=pltpu.VMEM),
            scratch_shapes=[
                pltpu.VMEM((keys, 2 * HD), BF),
                pltpu.VMEM((heads * n, 256), BF),
                pltpu.VMEM((heads * n, 256), F32),
                pltpu.VMEM((heads * n, 128), F32),
            ],
        ),
        out_shape=jax.ShapeDtypeStruct((n, width), BF),
        compiler_params=pltpu.CompilerParams(vmem_limit_bytes=24 * MIB),
        cost_estimate=pl.CostEstimate(
            flops=4 * heads * n * (keys + n) * 256,
            bytes_accessed=8 * 2**20,
            transcendentals=heads * n * (keys + n),
        ),
        name="attention",
    )(table, q, resp, pool)


def predict_kernel(x_ref, p_ref, out_ref, acc):
    k = pl.program_id(0)
    part = jnp.dot(x_ref[...], p_ref[...], preferred_element_type=F32)

    @pl.when(k == 0)
    def _():
        acc[...] = part

    @pl.when(k > 0)
    def _():
        acc[...] += part

    @pl.when(k == pl.num_programs(0) - 1)
    def _():
        out_ref[...] = acc[...].astype(BF)


def predict(x, p, block=1536):
    n, k = x.shape
    m = p.shape[1]
    return pl.pallas_call(
        predict_kernel,
        grid=(k // block,),
        in_specs=[
            pl.BlockSpec((n, block), lambda i: (0, i)),
            pl.BlockSpec((block, m), lambda i: (i, 0)),
        ],
        out_specs=pl.BlockSpec((n, m), lambda i: (0, 0)),
        out_shape=jax.ShapeDtypeStruct((n, m), BF),
        scratch_shapes=[pltpu.VMEM((n, m), F32)],
        compiler_params=pltpu.CompilerParams(vmem_limit_bytes=52 * MIB),
        cost_estimate=pl.CostEstimate(
            flops=2 * n * m * k, bytes_accessed=2 * (n * k + k * m + n * m), transcendentals=0
        ),
        name="predict",
    )(x, p)


def pick_kernel(routes, lengths, x_hbm, out_ref, x_ref, sem):
    mine = lax.axis_index("grp")
    _, _, _, h, x = coordinates()
    for z, c in ((0, 0), (0, 1), (1, 0), (1, 1)):
        row = pl.multiple_of((z * 8 + x * 2 + c) * 32, 32)
        there = x_ref.at[pl.ds((z * 2 + c) * 32, 32)]
        pltpu.make_async_copy(x_hbm.at[pl.ds(row, 32)], there, sem).start()
    token = lax.broadcasted_iota(jnp.int32, (32, 128), 0) * 128
    token += lax.broadcasted_iota(jnp.int32, (32, 128), 1)
    mark = jnp.full((32, 128), 127, jnp.int32)
    for r in range(16):
        route = routes[r]
        rank = jnp.int32(0)
        for earlier in range(r):
            rank += (routes[earlier] == route).astype(jnp.int32)
        dead = jnp.where(token % LMAX < lengths[mine, r], 0, 64)
        mark = jnp.where(token // LMAX == r, route * MOST + rank + dead, mark)
    mark = mark.astype(F32).astype(BF)
    pltpu.make_async_copy(x_ref, x_ref, sem).wait()

    for z, y, c in GRID:
        at = grp_at(z, y, c) * 32
        row = (z * 2 + c) * 32
        for i, zf in enumerate((1 - z, z)):
            block = zf * 8 + y * 2 + jnp.where(h == 0, 1 - c, c)
            col = pl.multiple_of(block * 384, 384)
            out_ref[at : at + 32, i * 384 : (i + 1) * 384] = x_ref[row : row + 32, pl.ds(col, 384)]
        out_ref[at : at + 32, 768:] = mark


def pick(routes, lengths, x):
    return pl.pallas_call(
        pick_kernel,
        grid_spec=pltpu.PrefetchScalarGridSpec(
            num_scalar_prefetch=2,
            grid=(),
            in_specs=[pl.BlockSpec(memory_space=pl.ANY)],
            out_specs=pl.BlockSpec(memory_space=pltpu.VMEM),
            scratch_shapes=[pltpu.VMEM((128, x.shape[1]), BF), pltpu.SemaphoreType.DMA(())],
        ),
        out_shape=jax.ShapeDtypeStruct((512, 896), BF),
        compiler_params=pltpu.CompilerParams(vmem_limit_bytes=58 * MIB),
        cost_estimate=pl.CostEstimate(flops=0, bytes_accessed=3 * 2**20, transcendentals=0),
        name="pick",
    )(routes, lengths, x)


def slot_of(mark):
    lane = lax.broadcasted_iota(jnp.int32, mark.shape, 1)
    return jnp.where(mark < 64, mark, mark - 64) * LMAX + lane % LMAX


def compact_kernel(x_ref, out_ref, meta_ref):
    z, _, c, _, x = coordinates()

    def marks_of(prompt):
        at = pl.multiple_of(prompt * 32, 32)
        rows = x_ref[pl.ds(at, 32), 768:].astype(F32)
        return jnp.concatenate([rows[0:1], rows[1:2]], 1).astype(jnp.int32)

    slot = slot_of(marks_of(z * 8 + x * 2 + c))
    rows = lax.broadcasted_iota(jnp.int32, (512, 256), 0)
    sel = (rows == slot).astype(F32).astype(BF)
    out_ref[...] = lax.dot_general(
        x_ref[:, :768], sel, (((0,), (0,)), ((), ())), preferred_element_type=F32
    ).astype(BF)

    every = x_ref[:, 768:].astype(F32)
    own = marks_of(lax.axis_index("grp"))
    weight = jnp.zeros(own.shape, F32)
    for s in range(16):
        hit = (every == 2.0 * s) | (every == 2.0 * s + 1.0)
        count = jnp.sum(jnp.sum(hit.astype(F32), axis=0, keepdims=True), axis=1, keepdims=True)
        weight = jnp.where((own == 2 * s) | (own == 2 * s + 1), 1.0 / count, weight)
    meta_ref[...] = jnp.concatenate(
        [slot_of(own).astype(F32), weight, jnp.zeros((6, 256), F32)], 0
    )


def compact(x):
    return pl.pallas_call(
        compact_kernel,
        in_specs=[pl.BlockSpec(memory_space=pltpu.VMEM)],
        out_specs=[pl.BlockSpec(memory_space=pltpu.VMEM)] * 2,
        out_shape=[
            jax.ShapeDtypeStruct((768, 256), BF),
            jax.ShapeDtypeStruct((8, 256), F32),
        ],
        compiler_params=pltpu.CompilerParams(vmem_limit_bytes=12 * MIB),
        cost_estimate=pl.CostEstimate(
            flops=2 * 512 * 768 * 256, bytes_accessed=2 * 2**20, transcendentals=0
        ),
        name="compact",
    )(x)


def grad_kernel(meta_ref, y_ref, tap_ref, out_ref):
    n = y_ref.shape[0]
    meta = meta_ref[...].T
    cols = lax.broadcasted_iota(jnp.int32, (256, n), 1)
    sel = (cols == meta[:, 0:1].astype(jnp.int32)).astype(F32).astype(BF)
    predicted = jnp.dot(sel, y_ref[...], preferred_element_type=F32)
    out_ref[...] = ((predicted - tap_ref[...].astype(F32)) * meta[:, 1:2]).astype(BF)


def grad_pred(meta, y, tap):
    return pl.pallas_call(
        grad_kernel,
        in_specs=[pl.BlockSpec(memory_space=pltpu.VMEM)] * 3,
        out_specs=pl.BlockSpec(memory_space=pltpu.VMEM),
        out_shape=jax.ShapeDtypeStruct(tap.shape, BF),
        compiler_params=pltpu.CompilerParams(vmem_limit_bytes=10 * MIB),
        cost_estimate=pl.CostEstimate(
            flops=2 * 512 * 256 * tap.shape[1], bytes_accessed=3 * 2**20, transcendentals=0
        ),
        name="grad_pred",
    )(meta, y, tap)


def first_kernel(*refs):
    xs, gs, (out_ref, send_ref, keep_ref, gbuf_ref) = refs[:8], refs[8:13], refs[13:]
    _, y, _, h, x = coordinates()
    for ref, dy, lo in zip(gs, (0, 1, 3, 2, 2), (0, 0, 0, 0, 128)):
        at = pl.multiple_of(((y + dy + 4 - x) % 4) * 256 + lo, 128)
        gbuf_ref[pl.ds(at, ref.shape[0]), :] = ref[...]
    for i in range(4):
        here = slice(i * 256, (i + 1) * 256)

        @pl.when(h == 0)
        def _():
            send_ref[:, here] = xs[i][...]
            keep_ref[:, here] = xs[4 + i][...]

        @pl.when(h == 1)
        def _():
            send_ref[:, here] = xs[4 + i][...]
            keep_ref[:, here] = xs[i][...]

    out_ref[...] = jnp.dot(
        send_ref[:384, :], gbuf_ref[...], preferred_element_type=F32
    ).astype(BF)


def outer_first(xs, gs):
    m = gs[0].shape[1]
    return pl.pallas_call(
        first_kernel,
        in_specs=[pl.BlockSpec(memory_space=pltpu.VMEM)] * 13,
        out_specs=[pl.BlockSpec(memory_space=pltpu.VMEM)] * 4,
        out_shape=[
            jax.ShapeDtypeStruct((384, m), BF),
            jax.ShapeDtypeStruct((768, 1024), BF),
            jax.ShapeDtypeStruct((768, 1024), BF),
            jax.ShapeDtypeStruct((1024, m), BF),
        ],
        compiler_params=pltpu.CompilerParams(vmem_limit_bytes=10 * MIB),
        cost_estimate=pl.CostEstimate(
            flops=2 * 768 * 1024 * m, bytes_accessed=8 * 2**20, transcendentals=0
        ),
        name="outer_first",
    )(*xs, *gs)


def rows_kernel(x_ref, g_ref, *refs, lo):
    added, out_ref = refs[:-1], refs[-1]
    rows = out_ref.shape[0]
    total = jnp.dot(x_ref[lo : lo + rows, :], g_ref[...], preferred_element_type=F32)
    for ref in added:
        total += ref[...].astype(F32)
    out_ref[...] = total.astype(out_ref.dtype)


def outer_rows(x, g, lo, dtype, *added):
    m = g.shape[1]
    return pl.pallas_call(
        functools.partial(rows_kernel, lo=lo),
        in_specs=[pl.BlockSpec(memory_space=pltpu.VMEM)] * (2 + len(added)),
        out_specs=pl.BlockSpec(memory_space=pltpu.VMEM),
        out_shape=jax.ShapeDtypeStruct((384, m), dtype),
        compiler_params=pltpu.CompilerParams(vmem_limit_bytes=10 * MIB),
        cost_estimate=pl.CostEstimate(
            flops=2 * 384 * 1024 * m, bytes_accessed=4 * 2**20, transcendentals=0
        ),
        name="outer_rows",
    )(x, g, *added)


def body(queries, responses, cache_pool, page_table, lengths, routes, student_rows, projection):
    rows = student_rows[0].reshape(-1, student_rows.shape[-1])
    share = pick(routes.reshape(-1), lengths, rows)
    share = lax.all_to_all(share, "grp", split_axis=0, concat_axis=0, tiled=True)

    predicted = predict(rows, projection)
    mine, meta = compact(share)
    predicted, mine = lax.optimization_barrier((predicted, mine))
    predicted = lax.all_to_all(predicted, "grp", split_axis=0, concat_axis=0, tiled=True)

    other = lax.ppermute(mine, "tp", H_SWAP)
    ma = lax.ppermute(mine, "tp", x_shift(1))
    mb = lax.ppermute(mine, "tp", x_shift(-1))
    mc = lax.ppermute(mine, "tp", x_shift(2))

    q = queries[0].reshape(256, -1)
    q, meta = lax.optimization_barrier((q, meta))
    tap = attention(q, responses[0].reshape(256, -1), cache_pool, page_table[0])
    g = grad_pred(meta, predicted, tap)
    ga = lax.ppermute(g, "grp", y_shift(1))
    gb = lax.ppermute(g, "grp", y_shift(-1))
    other, ma, mb, mc, g = lax.optimization_barrier((other, ma, mb, mc, g))
    oa = lax.ppermute(other, "tp", x_shift(1))
    ob = lax.ppermute(other, "tp", x_shift(-1))
    oc = lax.ppermute(other, "tp", x_shift(2))
    ga, gb, oa = lax.optimization_barrier((ga, gb, oa))
    gc = lax.ppermute(ga[:128], "grp", y_shift(1))
    gd = lax.ppermute(gb[128:], "grp", y_shift(-1))
    xs = (mine, mb, mc, ma, other, ob, oc, oa)

    send, sent_x, kept_x, grads = outer_first(xs, (g, gb, ga, gc, gd))
    got = lax.ppermute(send, "grp", C_SWAP)
    send = outer_rows(sent_x, grads, 384, BF)
    got_own = lax.ppermute(send, "grp", C_SWAP)
    to_z = outer_rows(kept_x, grads, 0, BF, got)
    stay = outer_rows(kept_x, grads, 384, F32, got_own)
    return (stay + lax.ppermute(to_z, "grp", Z_SWAP).astype(F32)).astype(BF)


def solution(mesh):
    return jax.shard_map(
        body,
        mesh=mesh,
        in_specs=(
            P("grp", None, None, "tp"),
            P("grp", None, None, "tp"),
            P("grp", None, "tp"),
            P("grp", None),
            P(),
            P("grp", None, None),
            P("grp", None, None, None),
            P(None, "tp"),
        ),
        out_specs=P("grp", "tp"),
        check_vma=False,
    )
```

```python
import functools

import jax
import jax.numpy as jnp
from jax import lax
from jax.experimental import pallas as pl
from jax.experimental.pallas import tpu as pltpu
from jax.sharding import PartitionSpec as P

HD = 192
MOST = 2
GQA = 6
PAGE = 64
LMAX = 16
LOG2E = 1.4426950408889634
BF = jnp.bfloat16
F32 = jnp.float32
MIB = 2**20

GRID = [(z, y, c) for z in range(2) for y in range(4) for c in range(2)]
TPGRID = [(h, x) for h in range(2) for x in range(4)]


def grp_at(z, y, c):
    return z * 8 + (y % 4) * 2 + c


def y_shift(step):
    return [(grp_at(z, y, c), grp_at(z, y + step, c)) for z, y, c in GRID]


Z_SWAP = [(grp_at(z, y, c), grp_at(1 - z, y, c)) for z, y, c in GRID]
C_SWAP = [(grp_at(z, y, c), grp_at(z, y, 1 - c)) for z, y, c in GRID]
H_SWAP = [(h * 4 + x, (1 - h) * 4 + x) for h, x in TPGRID]


def x_shift(step):
    return [(h * 4 + x, h * 4 + (x + step) % 4) for h, x in TPGRID]


def coordinates():
    g, t = lax.axis_index("grp"), lax.axis_index("tp")
    return g // 8, (g // 2) % 4, g % 2, t // 4, t % 4


def attention_kernel(
    table, q_ref, resp_hbm, pool_ref, out_ref, resp_ref, kv, q2, acc, tops, sem, *, chunk, mb
):
    resp_copy = pltpu.make_async_copy(resp_hbm, resp_ref, sem)
    resp_copy.start()
    pages = table.shape[0]
    n = q_ref.shape[0]
    heads = q_ref.shape[1] // HD
    scale = LOG2E * float(HD) ** -0.5
    pad = jnp.zeros((n, 256 - HD), BF)
    for i in range(heads):
        q2[i * n : (i + 1) * n, :] = jnp.concatenate([q_ref[:, i * HD : (i + 1) * HD], pad], 1)

    def fold(rows, first):
        kt = rows[:, 0:256].T
        values = rows[:, 128:384]
        lane = lax.broadcasted_iota(jnp.int32, values.shape, 1)
        vx = jnp.where(lane < 64, jnp.where(lane == 0, 1.0, 0.0).astype(BF), values)
        for lo in range(0, heads * n, mb):
            here = slice(lo, lo + mb)
            s = jnp.dot(q2[here, :], kt, preferred_element_type=F32)
            if first:
                row = lax.broadcasted_iota(jnp.int32, s.shape, 0) % n
                col = lax.broadcasted_iota(jnp.int32, s.shape, 1)
                s = jnp.where((row // LMAX == col // LMAX) & (col <= row), s, -1e30)
            new = jnp.max(s, axis=1, keepdims=True) * scale
            if not first:
                old = tops[here, 0:1]
                new = jnp.maximum(old, new)
            p = jnp.exp2(s * scale - new).astype(BF)
            o = jnp.dot(p, vx, preferred_element_type=F32)
            acc[here, :] = o if first else acc[here, :] * jnp.exp2(old - new) + o
            tops[here, :] = jnp.broadcast_to(new, (mb, 128))

    resp_copy.wait()
    fold(resp_ref[...], True)
    for lo in range(0, pages * PAGE, chunk):
        for j in range(lo // PAGE, (lo + chunk) // PAGE):
            kv[j * PAGE : (j + 1) * PAGE, :] = pool_ref[table[j]]
        fold(kv[lo : lo + chunk, :], False)
    for i in range(0, heads, 2):
        ratios = []
        for j in (i, i + 1):
            total = acc[j * n : (j + 1) * n, :]
            ratios.append(total[:, 64:] / total[:, 0:1])
        out_ref[:, i * HD : (i + 2) * HD] = jnp.concatenate(ratios, 1).astype(BF)


def attention(q, resp, pool, table, chunk=2048, mb=256):
    n, width = q.shape
    keys = table.shape[0] * PAGE
    heads = width // HD
    return pl.pallas_call(
        functools.partial(attention_kernel, chunk=chunk, mb=mb),
        grid_spec=pltpu.PrefetchScalarGridSpec(
            num_scalar_prefetch=1,
            grid=(),
            in_specs=[pl.BlockSpec(memory_space=m) for m in (pltpu.VMEM, pl.ANY, pltpu.VMEM)],
            out_specs=pl.BlockSpec(memory_space=pltpu.VMEM),
            scratch_shapes=[
                pltpu.VMEM(resp.shape, BF),
                pltpu.VMEM((keys, 2 * HD), BF),
                pltpu.VMEM((heads * n, 256), BF),
                pltpu.VMEM((heads * n, 256), F32),
                pltpu.VMEM((heads * n, 128), F32),
                pltpu.SemaphoreType.DMA(()),
            ],
        ),
        out_shape=jax.ShapeDtypeStruct((n, width), BF),
        compiler_params=pltpu.CompilerParams(vmem_limit_bytes=24 * MIB),
        cost_estimate=pl.CostEstimate(
            flops=4 * heads * n * (keys + n) * 256,
            bytes_accessed=8 * 2**20,
            transcendentals=heads * n * (keys + n),
        ),
        name="attention",
    )(table, q, resp, pool)


def predict_kernel(x_ref, p_ref, out_ref, acc):
    k = pl.program_id(0)
    part = jnp.dot(x_ref[...], p_ref[...], preferred_element_type=F32)

    @pl.when(k == 0)
    def _():
        acc[...] = part

    @pl.when(k > 0)
    def _():
        acc[...] += part

    @pl.when(k == pl.num_programs(0) - 1)
    def _():
        out_ref[...] = acc[...].astype(BF)


def predict(x, p, block=1536):
    n, k = x.shape
    m = p.shape[1]
    return pl.pallas_call(
        predict_kernel,
        grid=(k // block,),
        in_specs=[
            pl.BlockSpec((n, block), lambda i: (0, i)),
            pl.BlockSpec((block, m), lambda i: (i, 0)),
        ],
        out_specs=pl.BlockSpec((n, m), lambda i: (0, 0)),
        out_shape=jax.ShapeDtypeStruct((n, m), BF),
        scratch_shapes=[pltpu.VMEM((n, m), F32)],
        compiler_params=pltpu.CompilerParams(vmem_limit_bytes=52 * MIB),
        cost_estimate=pl.CostEstimate(
            flops=2 * n * m * k, bytes_accessed=2 * (n * k + k * m + n * m), transcendentals=0
        ),
        name="predict",
    )(x, p)


def pick_kernel(routes, lengths, x_hbm, out_ref, x_ref, sem):
    mine = lax.axis_index("grp")
    _, _, _, h, x = coordinates()
    for z, c in ((0, 0), (0, 1), (1, 0), (1, 1)):
        row = pl.multiple_of((z * 8 + x * 2 + c) * 32, 32)
        there = x_ref.at[pl.ds((z * 2 + c) * 32, 32)]
        pltpu.make_async_copy(x_hbm.at[pl.ds(row, 32)], there, sem).start()
    token = lax.broadcasted_iota(jnp.int32, (32, 128), 0) * 128
    token += lax.broadcasted_iota(jnp.int32, (32, 128), 1)
    mark = jnp.full((32, 128), 127, jnp.int32)
    for r in range(16):
        route = routes[r]
        rank = jnp.int32(0)
        for earlier in range(r):
            rank += (routes[earlier] == route).astype(jnp.int32)
        dead = jnp.where(token % LMAX < lengths[mine, r], 0, 64)
        mark = jnp.where(token // LMAX == r, route * MOST + rank + dead, mark)
    mark = mark.astype(F32).astype(BF)
    pltpu.make_async_copy(x_ref, x_ref, sem).wait()

    for z, y, c in GRID:
        at = grp_at(z, y, c) * 32
        row = (z * 2 + c) * 32
        for i, zf in enumerate((1 - z, z)):
            block = zf * 8 + y * 2 + jnp.where(h == 0, 1 - c, c)
            col = pl.multiple_of(block * 384, 384)
            out_ref[at : at + 32, i * 384 : (i + 1) * 384] = x_ref[row : row + 32, pl.ds(col, 384)]
        out_ref[at : at + 32, 768:] = mark


def pick(routes, lengths, x):
    return pl.pallas_call(
        pick_kernel,
        grid_spec=pltpu.PrefetchScalarGridSpec(
            num_scalar_prefetch=2,
            grid=(),
            in_specs=[pl.BlockSpec(memory_space=pl.ANY)],
            out_specs=pl.BlockSpec(memory_space=pltpu.VMEM),
            scratch_shapes=[pltpu.VMEM((128, x.shape[1]), BF), pltpu.SemaphoreType.DMA(())],
        ),
        out_shape=jax.ShapeDtypeStruct((512, 896), BF),
        compiler_params=pltpu.CompilerParams(vmem_limit_bytes=58 * MIB),
        cost_estimate=pl.CostEstimate(flops=0, bytes_accessed=3 * 2**20, transcendentals=0),
        name="pick",
    )(routes, lengths, x)


def slot_of(mark):
    lane = lax.broadcasted_iota(jnp.int32, mark.shape, 1)
    return jnp.where(mark < 64, mark, mark - 64) * LMAX + lane % LMAX


def compact_kernel(x_ref, out_ref, meta_ref):
    z, _, c, _, x = coordinates()

    def marks_of(prompt):
        at = pl.multiple_of(prompt * 32, 32)
        rows = x_ref[pl.ds(at, 32), 768:].astype(F32)
        return jnp.concatenate([rows[0:1], rows[1:2]], 1).astype(jnp.int32)

    slot = slot_of(marks_of(z * 8 + x * 2 + c))
    rows = lax.broadcasted_iota(jnp.int32, (512, 256), 0)
    sel = (rows == slot).astype(F32).astype(BF)
    out_ref[...] = lax.dot_general(
        x_ref[:, :768], sel, (((0,), (0,)), ((), ())), preferred_element_type=F32
    ).astype(BF)

    every = x_ref[:, 768:].astype(F32)
    own = marks_of(lax.axis_index("grp"))
    weight = jnp.zeros(own.shape, F32)
    for s in range(16):
        hit = (every == 2.0 * s) | (every == 2.0 * s + 1.0)
        count = jnp.sum(jnp.sum(hit.astype(F32), axis=0, keepdims=True), axis=1, keepdims=True)
        weight = jnp.where((own == 2 * s) | (own == 2 * s + 1), 1.0 / count, weight)
    meta_ref[...] = jnp.concatenate(
        [slot_of(own).astype(F32), weight, jnp.zeros((6, 256), F32)], 0
    )


def compact(x):
    return pl.pallas_call(
        compact_kernel,
        in_specs=[pl.BlockSpec(memory_space=pltpu.VMEM)],
        out_specs=[pl.BlockSpec(memory_space=pltpu.VMEM)] * 2,
        out_shape=[
            jax.ShapeDtypeStruct((768, 256), BF),
            jax.ShapeDtypeStruct((8, 256), F32),
        ],
        compiler_params=pltpu.CompilerParams(vmem_limit_bytes=12 * MIB),
        cost_estimate=pl.CostEstimate(
            flops=2 * 512 * 768 * 256, bytes_accessed=2 * 2**20, transcendentals=0
        ),
        name="compact",
    )(x)


def grad_kernel(meta_ref, y_ref, tap_ref, out_ref):
    n = y_ref.shape[0]
    meta = meta_ref[...].T
    cols = lax.broadcasted_iota(jnp.int32, (256, n), 1)
    sel = (cols == meta[:, 0:1].astype(jnp.int32)).astype(F32).astype(BF)
    predicted = jnp.dot(sel, y_ref[...], preferred_element_type=F32)
    out_ref[...] = ((predicted - tap_ref[...].astype(F32)) * meta[:, 1:2]).astype(BF)


def grad_pred(meta, y, tap):
    return pl.pallas_call(
        grad_kernel,
        in_specs=[pl.BlockSpec(memory_space=pltpu.VMEM)] * 3,
        out_specs=pl.BlockSpec(memory_space=pltpu.VMEM),
        out_shape=jax.ShapeDtypeStruct(tap.shape, BF),
        compiler_params=pltpu.CompilerParams(vmem_limit_bytes=10 * MIB),
        cost_estimate=pl.CostEstimate(
            flops=2 * 512 * 256 * tap.shape[1], bytes_accessed=3 * 2**20, transcendentals=0
        ),
        name="grad_pred",
    )(meta, y, tap)


def first_kernel(*refs):
    xs, gs, (out_ref, send_ref, keep_ref, gbuf_ref) = refs[:8], refs[8:13], refs[13:]
    _, y, _, h, x = coordinates()
    for ref, dy, lo in zip(gs, (0, 1, 3, 2, 2), (0, 0, 0, 0, 128)):
        at = pl.multiple_of(((y + dy + 4 - x) % 4) * 256 + lo, 128)
        gbuf_ref[pl.ds(at, ref.shape[0]), :] = ref[...]
    for i in range(4):
        here = slice(i * 256, (i + 1) * 256)

        @pl.when(h == 0)
        def _():
            send_ref[:, here] = xs[i][...]
            keep_ref[:, here] = xs[4 + i][...]

        @pl.when(h == 1)
        def _():
            send_ref[:, here] = xs[4 + i][...]
            keep_ref[:, here] = xs[i][...]

    out_ref[...] = jnp.dot(
        send_ref[:384, :], gbuf_ref[...], preferred_element_type=F32
    ).astype(BF)


def outer_first(xs, gs):
    m = gs[0].shape[1]
    return pl.pallas_call(
        first_kernel,
        in_specs=[pl.BlockSpec(memory_space=pltpu.VMEM)] * 13,
        out_specs=[pl.BlockSpec(memory_space=pltpu.VMEM)] * 4,
        out_shape=[
            jax.ShapeDtypeStruct((384, m), BF),
            jax.ShapeDtypeStruct((768, 1024), BF),
            jax.ShapeDtypeStruct((768, 1024), BF),
            jax.ShapeDtypeStruct((1024, m), BF),
        ],
        compiler_params=pltpu.CompilerParams(vmem_limit_bytes=10 * MIB),
        cost_estimate=pl.CostEstimate(
            flops=2 * 768 * 1024 * m, bytes_accessed=8 * 2**20, transcendentals=0
        ),
        name="outer_first",
    )(*xs, *gs)


def rows_kernel(x_ref, g_ref, *refs, lo):
    added, out_ref = refs[:-1], refs[-1]
    rows = out_ref.shape[0]
    total = jnp.dot(x_ref[lo : lo + rows, :], g_ref[...], preferred_element_type=F32)
    for ref in added:
        total += ref[...].astype(F32)
    out_ref[...] = total.astype(out_ref.dtype)


def outer_rows(x, g, lo, dtype, *added):
    m = g.shape[1]
    return pl.pallas_call(
        functools.partial(rows_kernel, lo=lo),
        in_specs=[pl.BlockSpec(memory_space=pltpu.VMEM)] * (2 + len(added)),
        out_specs=pl.BlockSpec(memory_space=pltpu.VMEM),
        out_shape=jax.ShapeDtypeStruct((384, m), dtype),
        compiler_params=pltpu.CompilerParams(vmem_limit_bytes=10 * MIB),
        cost_estimate=pl.CostEstimate(
            flops=2 * 384 * 1024 * m, bytes_accessed=4 * 2**20, transcendentals=0
        ),
        name="outer_rows",
    )(x, g, *added)


def body(queries, responses, cache_pool, page_table, lengths, routes, student_rows, projection):
    rows = student_rows[0].reshape(-1, student_rows.shape[-1])
    share = pick(routes.reshape(-1), lengths, rows)
    share = lax.all_to_all(share, "grp", split_axis=0, concat_axis=0, tiled=True)

    predicted = predict(rows, projection)
    mine, meta = compact(share)
    predicted, mine = lax.optimization_barrier((predicted, mine))
    predicted = lax.all_to_all(predicted, "grp", split_axis=0, concat_axis=0, tiled=True)

    other = lax.ppermute(mine, "tp", H_SWAP)
    ma = lax.ppermute(mine, "tp", x_shift(1))
    mb = lax.ppermute(mine, "tp", x_shift(-1))
    mc = lax.ppermute(mine, "tp", x_shift(2))

    q = queries[0].reshape(256, -1)
    q, meta = lax.optimization_barrier((q, meta))
    tap = attention(q, responses[0].reshape(256, -1), cache_pool, page_table[0])
    g = grad_pred(meta, predicted, tap)
    ga = lax.ppermute(g, "grp", y_shift(1))
    gb = lax.ppermute(g, "grp", y_shift(-1))
    other, ma, mb, mc, g = lax.optimization_barrier((other, ma, mb, mc, g))
    oa = lax.ppermute(other, "tp", x_shift(1))
    ob = lax.ppermute(other, "tp", x_shift(-1))
    oc = lax.ppermute(other, "tp", x_shift(2))
    ga, gb, oa = lax.optimization_barrier((ga, gb, oa))
    gc = lax.ppermute(ga[:128], "grp", y_shift(1))
    gd = lax.ppermute(gb[128:], "grp", y_shift(-1))
    xs = (mine, mb, mc, ma, other, ob, oc, oa)

    send, sent_x, kept_x, grads = outer_first(xs, (g, gb, ga, gc, gd))
    got = lax.ppermute(send, "grp", C_SWAP)
    send = outer_rows(sent_x, grads, 384, BF)
    got_own = lax.ppermute(send, "grp", C_SWAP)
    to_z = outer_rows(kept_x, grads, 0, BF, got)
    stay = outer_rows(kept_x, grads, 384, F32, got_own)
    return (stay + lax.ppermute(to_z, "grp", Z_SWAP).astype(F32)).astype(BF)


def solution(mesh):
    return jax.shard_map(
        body,
        mesh=mesh,
        in_specs=(
            P("grp", None, None, "tp"),
            P("grp", None, None, "tp"),
            P("grp", None, "tp"),
            P("grp", None),
            P(),
            P("grp", None, None),
            P("grp", None, None, None),
            P(None, "tp"),
        ),
        out_specs=P("grp", "tp"),
        check_vma=False,
    )
```
